128 devices in a mesh: gx: 8 (over x_lo, z), gy: 16 (over x_hi, y, core).
Axes of the slice: x: 4 (x_hi: 2, x_lo: 2; x = x_hi * 2 + x_lo), y: 4, z: 4, core: 2. Of those that a mesh axis runs over, the one named last changes fastest.
Arguments:
- intensity: float32 [52, 1024, 2048], P(None, 'gx', 'gy'), may hold values from -300 to 300
Outputs:
- tensor_field: float32 [6, 4, 1024, 2048], P(None, None, 'gx', 'gy')
The draws below stay inside these ranges and needn't reach their ends.
All inputs are finite; a program needn't handle non-finite values.
Results may differ from the reference program's by a relative error of at most 0.00002.
Values sent between devices are 32-bit elements; how exact they have to be, the bound alone decides.
A program may use at most 192 MiB of HBM per device.

```python
import math
import jax
import jax.numpy as jnp
from jax import lax

RD = 6
RI = 18
ZIN = 52
NX = 1024
NY = 2048


def levels(stream_key, shape, split, least, largest):
    def one(position, parts):
        steps = jax.random.uniform(jax.random.fold_in(jax.random.fold_in(stream_key, 6), position), (parts,), jnp.float32, least / len(split), largest / len(split))
        return jnp.repeat(jnp.exp(steps), shape[position] // parts).reshape((-1,) + (1,) * (len(shape) - position - 1))

    loudness = one(*split[0])
    for cut in split[1:]:
        loudness = loudness * one(*cut)
    return loudness


def gaussian(key, shape, scale, most, shards=(), dtype=jnp.bfloat16):
    level = levels(key, shape, shards, -0.22, 0.18) if shards else 1.0
    array = jax.random.normal(key, shape, jnp.float32) * scale * level
    return jnp.minimum(jnp.maximum(array, -most), most).astype(dtype)


def setup_inputs(seed: int = 0) -> dict:
    key_of = jax.random.split(jax.random.key(seed), 2)
    intensity = gaussian(key_of[0], (ZIN, NX, NY), 50.0, 300.0, ((1, 8), (2, 16)), jnp.float32)
    return {"intensity": intensity}


def gauss_taps(sigma, radius):
    values = [math.exp(-k * k / (2.0 * sigma * sigma)) for k in range(-radius, radius + 1)]
    total = sum(values)
    return [v / total for v in values]


def deriv_taps(sigma, radius):
    smooth = gauss_taps(sigma, radius)
    return [(k - radius) / (sigma * sigma) * smooth[k] for k in range(2 * radius + 1)]


def slide(field, kernel_taps, axis):
    count = field.shape[axis] - len(kernel_taps) + 1
    total = kernel_taps[0] * lax.slice_in_dim(field, 0, count, axis=axis)
    for index in range(1, len(kernel_taps)):
        total = total + kernel_taps[index] * lax.slice_in_dim(field, index, index + count, axis=axis)
    return total


def reference(intensity):
    smooth_d = gauss_taps(2.0, RD)
    deriv_d = deriv_taps(2.0, RD)
    smooth_i = gauss_taps(6.0, RI)
    padded = jnp.pad(intensity, ((0, 0), (RD, RD), (RD, RD)))
    along_y = slide(padded, smooth_d, 2)
    grad_z = slide(slide(along_y, smooth_d, 1), deriv_d, 0)
    grad_x = slide(slide(along_y, deriv_d, 1), smooth_d, 0)
    grad_y = slide(slide(slide(padded, deriv_d, 2), smooth_d, 1), smooth_d, 0)
    pairs = [(grad_x, grad_x), (grad_x, grad_y), (grad_x, grad_z), (grad_y, grad_y), (grad_y, grad_z), (grad_z, grad_z)]
    results = []
    for first, second in pairs:
        flat = slide(first * second, smooth_i, 0)
        flat = jnp.pad(flat, ((0, 0), (RI, RI), (RI, RI)))
        results.append(slide(slide(flat, smooth_i, 1), smooth_i, 2))
    return jnp.stack(results, axis=0)
```

```python
import functools
import math

import jax
import jax.numpy as jnp
import ml_dtypes
import numpy as np
from jax import lax
from jax.experimental import pallas as pl
from jax.experimental.pallas import tpu as pltpu
from jax.sharding import PartitionSpec as P

RD = 6
RI = 18
ZIN = 52
ZG = ZIN - 2 * RD
ZO = ZG - 2 * RI
T = 128
H1 = 8
H2 = 24
X1 = T + 2 * H1
X2 = T + 2 * H2
S2 = 21
MESH = pl.DeviceIdType.MESH


def gauss_taps(sigma, radius):
    values = [math.exp(-k * k / (2.0 * sigma * sigma)) for k in range(-radius, radius + 1)]
    total = sum(values)
    return [v / total for v in values]


def deriv_taps(sigma, radius):
    smooth = gauss_taps(sigma, radius)
    return [(k - radius) / (sigma * sigma) * smooth[k] for k in range(2 * radius + 1)]


def banded(positions, taps, count):
    radius = len(taps) // 2
    out = np.zeros((len(positions), count), np.float64)
    for row, pos in enumerate(positions):
        if pos is None:
            continue
        for col in range(max(0, pos - radius), min(count, pos + radius + 1)):
            out[row, col] = taps[pos - col + radius]
    return out


def split_const(matrix):
    high = matrix.astype(ml_dtypes.bfloat16)
    low = (matrix - high.astype(np.float64)).astype(ml_dtypes.bfloat16)
    return jnp.asarray(high), jnp.asarray(low)


def weights():
    g2, d2, g6 = gauss_taps(2.0, RD), deriv_taps(2.0, RD), gauss_taps(6.0, RI)
    own = list(range(T))
    pos = own + list(range(-8, 0)) + list(range(T, T + 8))
    pos += [None] * (256 - len(pos))
    wy = np.concatenate([banded(pos, g2, T), banded(pos, d2, T)], axis=1)
    pos = own + list(range(-RI, 0)) + [None] * (S2 - RI) + list(range(T, T + RI))
    pos += [None] * (256 - len(pos))
    sy = banded(pos, g6, T)
    sx = banded(list(range(-H2, T + H2)), g6, T).T
    return split_const(wy) + split_const(sy) + split_const(sx)


def split(value):
    high = value.astype(jnp.bfloat16)
    low = (value - high.astype(jnp.float32)).astype(jnp.bfloat16)
    return high, low


def mm(a, b):
    return jnp.dot(a, b, preferred_element_type=jnp.float32)


def fsym(taps, values):
    r = len(taps) // 2
    total = taps[r] * values[r]
    for k in range(r):
        total = total + taps[k] * (values[k] + values[2 * r - k])
    return total


def fanti(taps, values):
    r = len(taps) // 2
    total = taps[2 * r] * (values[2 * r] - values[0])
    for k in range(1, r):
        total = total + taps[2 * r - k] * (values[2 * r - k] - values[k])
    return total


def kernel(nx, ny, i_ref, wyh, wyl, syh, syl, sxh, sxl, o_ref,
           iext, p1s, p1r, yg, yd, a1, a2, a3, fext, p2s, p2r, ysm,
           lsem, ssem, rsem):
    gx, gy = lax.axis_index("gx"), lax.axis_index("gy")
    g2, d2, g6 = gauss_taps(2.0, RD), deriv_taps(2.0, RD), gauss_taps(6.0, RI)
    has = {-1: gx > 0, 1: gx < nx - 1}
    hasy = {-1: gy > 0, 1: gy < ny - 1}
    dirs = [(dx, dy) for dx in (-1, 0, 1) for dy in (-1, 0, 1) if dx or dy]

    def exists(dx, dy):
        cond = None
        if dx:
            cond = has[dx]
        if dy:
            cond = hasy[dy] if cond is None else jnp.logical_and(cond, hasy[dy])
        return cond

    local = pltpu.make_async_copy(i_ref, iext.at[:, H1:H1 + T, :], lsem)
    local.start()

    barrier = pltpu.get_barrier_semaphore()
    for dx, dy in dirs:
        @pl.when(exists(dx, dy))
        def _():
            pl.semaphore_signal(barrier, inc=1, device_id=(gx + dx, gy + dy), device_id_type=MESH)
    kx = jnp.where(gx > 0, 1, 0) + jnp.where(gx < nx - 1, 1, 0)
    ky = jnp.where(gy > 0, 1, 0) + jnp.where(gy < ny - 1, 1, 0)
    pl.semaphore_wait(barrier, (kx + 1) * (ky + 1) - 1)

    def copies(stage):
        out = []
        for n, (dx, dy) in enumerate(dirs):
            halo, rows = (H1, X1) if stage == 0 else (H2, X2)
            main, send, recv = (iext, p1s, p1r) if stage == 0 else (fext, p2s, p2r)
            own = {-1: (halo, halo), 0: (halo, T), 1: (T, halo)}[dx]
            land = {-1: (T + halo, halo), 0: (halo, T), 1: (0, halo)}[dx]
            if dy == 0:
                src = main.at[:, pl.ds(own[0], own[1]), :]
                dst = main.at[:, pl.ds(land[0], land[1]), :]
            else:
                side = 0 if dy == 1 else 1
                src = send.at[side, :, pl.ds(own[0] - halo, own[1]), :]
                dst = recv.at[side, :, pl.ds(land[0], land[1]), :]
            k = stage * 8 + n
            out.append(((dx, dy), pltpu.make_async_remote_copy(
                src_ref=src, dst_ref=dst, send_sem=ssem.at[k], recv_sem=rsem.at[k],
                device_id=(gx + dx, gy + dy), device_id_type=MESH)))
        return out

    def start(stage, which):
        for (dx, dy), copy in copies(stage):
            if which(dx, dy):
                @pl.when(exists(dx, dy))
                def _():
                    copy.start()

    def finish(stage):
        halo = H1 if stage == 0 else H2
        main, recv = (iext, p1r) if stage == 0 else (fext, p2r)
        for (dx, dy), copy in copies(stage):
            @pl.when(exists(dx, dy))
            def _():
                copy.wait_send()
        for (dx, dy), copy in copies(stage):
            @pl.when(exists(-dx, -dy))
            def _():
                copy.wait_recv()

            @pl.when(jnp.logical_not(exists(-dx, -dy)))
            def _():
                land = {-1: (T + halo, halo), 0: (halo, T), 1: (0, halo)}[dx]
                if dy == 0:
                    main[:, pl.ds(land[0], land[1]), :] = jnp.zeros((main.shape[0], land[1], T), jnp.float32)
                else:
                    side = 0 if dy == 1 else 1
                    recv[side, :, pl.ds(land[0], land[1]), :] = jnp.zeros((recv.shape[1], land[1], T), jnp.float32)

    lane = lax.broadcasted_iota(jnp.int32, (8, T), 1)

    local.wait()
    start(0, lambda dx, dy: dy == 0)

    @pl.loop(0, T // 8)
    def _(t):
        row = pl.multiple_of(t * 8, 8)
        for g in range(4):
            right = jnp.zeros((8, T), jnp.float32)
            left = jnp.zeros((8, T), jnp.float32)
            for s in range(min(16, ZIN - 16 * g)):
                v = iext[16 * g + s, pl.ds(H1 + row, 8), :]
                mask = jnp.logical_and(lane >= 8 * s, lane < 8 * s + 8)
                right = jnp.where(mask, pltpu.roll(v, (8 * s + 8) % T, 1), right)
                left = jnp.where(mask, pltpu.roll(v, 8 * s, 1) if s else v, left)
            p1s[0, g, pl.ds(row, 8), :] = right
            p1s[1, g, pl.ds(row, 8), :] = left

    start(0, lambda dx, dy: dy != 0)
    finish(0)

    lane1 = lax.broadcasted_iota(jnp.int32, (X1, T), 1)
    for g in range(4):
        @pl.loop(0, min(16, ZIN - 16 * g))
        def _(s):
            z = 16 * g + s
            pleft = pltpu.roll(p1r[0, g], lax.rem(T - 8 * s, T), 1)
            pright = pltpu.roll(p1r[1, g], lax.rem(T + 8 - 8 * s, T), 1)
            u = jnp.where(lane1 < 8, pleft, jnp.where(lane1 < 16, pright, 0.0))
            high, low = split(jnp.concatenate([iext[z], u], axis=1))
            r = mm(high, wyh[...]) + mm(low, wyh[...]) + mm(high, wyl[...])
            yg[z] = r[:, :T]
            yd[z] = r[:, T:]

    @pl.loop(0, X1 // 8)
    def _(t):
        row = pl.ds(pl.multiple_of(t * 8, 8), 8)
        v = [yg[z, row, :] for z in range(2 * RD)]
        for z in range(ZG):
            v.append(yg[z + 2 * RD, row, :])
            w = v[z:z + 2 * RD + 1]
            a1[z, row, :] = fsym(g2, w)
            a2[z, row, :] = fanti(d2, w)
        v = [yd[z, row, :] for z in range(2 * RD)]
        for z in range(ZG):
            v.append(yd[z + 2 * RD, row, :])
            a3[z, row, :] = fsym(g2, v[z:z + 2 * RD + 1])

    @pl.loop(0, T // 8)
    def _(t):
        base = t * 8 + H1 - RD
        acc = [[None] * ZO for _ in range(6)]
        for z in range(ZG):
            gxv = fanti(d2, [a1[z, pl.ds(base + k, 8), :] for k in range(13)])
            gyv = fsym(g2, [a3[z, pl.ds(base + k, 8), :] for k in range(13)])
            gzv = fsym(g2, [a2[z, pl.ds(base + k, 8), :] for k in range(13)])
            prods = [gxv * gxv, gxv * gyv, gxv * gzv, gyv * gyv, gyv * gzv, gzv * gzv]
            for j in range(ZO):
                if 0 <= z - j <= 2 * RI:
                    for c in range(6):
                        term = g6[z - j] * prods[c]
                        acc[c][j] = term if acc[c][j] is None else acc[c][j] + term
        row = pl.ds(pl.multiple_of(t * 8, 8) + H2, 8)
        row0 = pl.ds(pl.multiple_of(t * 8, 8), 8)
        for j in range(ZO):
            right = jnp.zeros((8, T), jnp.float32)
            left = jnp.zeros((8, T), jnp.float32)
            for c in range(6):
                v = acc[c][j]
                fext[j * 6 + c, row, :] = v
                mask = jnp.logical_and(lane >= S2 * c, lane < S2 * c + RI)
                right = jnp.where(mask, pltpu.roll(v, (S2 * c + RI) % T, 1), right)
                left = jnp.where(mask, pltpu.roll(v, S2 * c, 1) if c else v, left)
            p2s[0, j, row0, :] = right
            p2s[1, j, row0, :] = left

    start(1, lambda dx, dy: True)
    finish(1)

    lane2 = lax.broadcasted_iota(jnp.int32, (X2, T), 1)
    for c in range(6):
        @pl.loop(0, ZO)
        def _(j):
            n = j * 6 + c
            pleft = p2r[0, j]
            if c:
                pleft = pltpu.roll(pleft, T - S2 * c, 1)
            pright = pltpu.roll(p2r[1, j], (T + S2 - S2 * c) % T, 1) if c != 1 else p2r[1, j]
            u = jnp.where(lane2 < S2, pleft, jnp.where(lane2 < 2 * S2, pright, 0.0))
            high, low = split(jnp.concatenate([fext[n], u], axis=1))
            ysm[n] = mm(high, syh[...]) + mm(low, syh[...]) + mm(high, syl[...])

    @pl.loop(0, ZO)
    def _(j):
        for c in range(0, 6, 2):
            high, low = split(jnp.concatenate([ysm[j * 6 + c], ysm[j * 6 + c + 1]], axis=1))
            r = mm(sxh[...], high) + mm(sxh[...], low) + mm(sxl[...], high)
            o_ref[c, j] = r[:, :T]
            o_ref[c + 1, j] = r[:, T:]


def shards(intensity):
    nx, ny = lax.axis_size("gx"), lax.axis_size("gy")
    f32 = jnp.float32
    vmem = pl.BlockSpec(memory_space=pltpu.VMEM)
    return pl.pallas_call(
        functools.partial(kernel, nx, ny),
        out_shape=jax.ShapeDtypeStruct((6, ZO, T, T), f32),
        in_specs=[pl.BlockSpec(memory_space=pl.ANY)] + [vmem] * 6,
        out_specs=vmem,
        scratch_shapes=[
            pltpu.VMEM((ZIN, X1, T), f32),
            pltpu.VMEM((2, 4, T, T), f32),
            pltpu.VMEM((2, 4, X1, T), f32),
            pltpu.VMEM((ZIN, X1, T), f32),
            pltpu.VMEM((ZIN, X1, T), f32),
            pltpu.VMEM((ZG, X1, T), f32),
            pltpu.VMEM((ZG, X1, T), f32),
            pltpu.VMEM((ZG, X1, T), f32),
            pltpu.VMEM((6 * ZO, X2, T), f32),
            pltpu.VMEM((2, ZO, T, T), f32),
            pltpu.VMEM((2, ZO, X2, T), f32),
            pltpu.VMEM((6 * ZO, X2, T), f32),
            pltpu.SemaphoreType.DMA,
            pltpu.SemaphoreType.DMA((16,)),
            pltpu.SemaphoreType.DMA((16,)),
        ],
        compiler_params=pltpu.CompilerParams(
            collective_id=0, has_side_effects=True, vmem_limit_bytes=56 * 1024 * 1024),
        cost_estimate=pl.CostEstimate(flops=4_000_000_000, bytes_accessed=6_000_000, transcendentals=0),
        name="structure_tensor",
    )(intensity, *weights())


def solution(mesh):
    in_specs = (P(None, "gx", "gy"),)
    out_specs = P(None, None, "gx", "gy")
    return jax.shard_map(shards, mesh=mesh, in_specs=in_specs, out_specs=out_specs, check_vma=False)
```

```python
import functools
import math

import jax
import jax.numpy as jnp
import ml_dtypes
import numpy as np
from jax import lax
from jax.experimental import pallas as pl
from jax.experimental.pallas import tpu as pltpu
from jax.sharding import PartitionSpec as P

RD = 6
RI = 18
ZIN = 52
ZG = ZIN - 2 * RD
ZO = ZG - 2 * RI
T = 128
H1 = 8
H2 = 24
X1 = T + 2 * H1
X2 = T + 2 * H2
S2 = 21
MESH = pl.DeviceIdType.MESH


def gauss_taps(sigma, radius):
    values = [math.exp(-k * k / (2.0 * sigma * sigma)) for k in range(-radius, radius + 1)]
    total = sum(values)
    return [v / total for v in values]


def deriv_taps(sigma, radius):
    smooth = gauss_taps(sigma, radius)
    return [(k - radius) / (sigma * sigma) * smooth[k] for k in range(2 * radius + 1)]


def banded(positions, taps, count):
    radius = len(taps) // 2
    out = np.zeros((len(positions), count), np.float64)
    for row, pos in enumerate(positions):
        if pos is None:
            continue
        for col in range(max(0, pos - radius), min(count, pos + radius + 1)):
            out[row, col] = taps[pos - col + radius]
    return out


def split_const(matrix):
    high = matrix.astype(ml_dtypes.bfloat16)
    low = (matrix - high.astype(np.float64)).astype(ml_dtypes.bfloat16)
    return jnp.asarray(high), jnp.asarray(low)


def blocks(inside, outside, taps, count):
    radius = len(taps) // 2
    block = np.array([[taps[p - q + radius] if abs(p - q) <= radius else 0.0 for q in outside] for p in inside])
    out = np.zeros((T, T), np.float64)
    for k in range(count):
        n = len(inside)
        out[n * k:n * k + n, n * k:n * k + n] = block
    return out


def stacked(matrix):
    high, low = split_const(matrix)
    return jnp.concatenate([high, high], axis=0), low


def weights():
    g2, d2, g6 = gauss_taps(2.0, RD), deriv_taps(2.0, RD), gauss_taps(6.0, RI)
    own = list(range(T))
    wy = np.concatenate([banded(own, g2, T), banded(own, d2, T)], axis=1)
    near = list(range(-8, 0)) + list(range(T, T + 8))
    edge = list(range(T - 8, T)) + list(range(8))
    we = np.concatenate([blocks(near, edge, g2, 8), blocks(near, edge, d2, 8)], axis=1)
    sy = banded(own, g6, T)
    near = list(range(-S2, 0)) + list(range(T, T + S2))
    edge = list(range(T - S2, T)) + list(range(S2))
    se = blocks(near, edge, g6, 3)
    sx = banded(list(range(-H2, T + H2)), g6, T).T
    return stacked(wy) + stacked(we) + stacked(sy) + stacked(se) + split_const(sx)


def split(value):
    high = value.astype(jnp.bfloat16)
    low = (value - high.astype(jnp.float32)).astype(jnp.bfloat16)
    return high, low


def mm(a, b):
    return jnp.dot(a, b, preferred_element_type=jnp.float32)


def mm2(high, low, weight2, weight_low):
    return mm(jnp.concatenate([high, low], axis=1), weight2) + mm(high, weight_low)


def fsym(taps, values):
    r = len(taps) // 2
    total = taps[r] * values[r]
    for k in range(r):
        total = total + taps[k] * (values[k] + values[2 * r - k])
    return total


def fanti(taps, values):
    r = len(taps) // 2
    total = taps[2 * r] * (values[2 * r] - values[0])
    for k in range(1, r):
        total = total + taps[2 * r - k] * (values[2 * r - k] - values[k])
    return total


def kernel(nx, ny, i_ref, wyh, wyl, weh, wel, syh, syl, seh, sel, sxh, sxl, o_ref,
           iext, s1s, s1r, c1s, c1r, aux, zg0, zd0, zg1, zd1, a1, a2, a3, e1, e2, e3,
           fext, s2s, s2r, lsem, ssem, rsem):
    gx, gy = lax.axis_index("gx"), lax.axis_index("gy")
    g2, d2, g6 = gauss_taps(2.0, RD), deriv_taps(2.0, RD), gauss_taps(6.0, RI)
    has = {-1: gx > 0, 1: gx < nx - 1}
    hasy = {-1: gy > 0, 1: gy < ny - 1}
    dirs = [(dx, dy) for dx in (-1, 0, 1) for dy in (-1, 0, 1) if dx or dy]
    f32 = jnp.float32

    def exists(dx, dy):
        cond = None
        if dx:
            cond = has[dx]
        if dy:
            cond = hasy[dy] if cond is None else jnp.logical_and(cond, hasy[dy])
        return cond

    local = pltpu.make_async_copy(i_ref, iext.at[:, H1:H1 + T, :], lsem)
    local.start()

    barrier = pltpu.get_barrier_semaphore()
    for dx, dy in dirs:
        @pl.when(exists(dx, dy))
        def _():
            pl.semaphore_signal(barrier, inc=1, device_id=(gx + dx, gy + dy), device_id_type=MESH)

    def ends(stage, dx, dy):
        if stage == 0:
            own, land = {-1: (H1, T + H1), 1: (T, 0), 0: (0, 0)}[dx]
            if dy == 0:
                return iext.at[:, pl.ds(own, H1), :], iext.at[:, pl.ds(land, H1), :]
            if dx == 0:
                side = 0 if dy == 1 else 1
                return s1s.at[side], s1r.at[side]
            end = 0 if dx == -1 else 1
            return c1s.at[end], c1r.at[1 - end, 0 if dy == 1 else 1]
        own, land, count = {-1: (0, T + H2, H2), 1: (T - H2, 0, H2), 0: (0, H2, T)}[dx]
        if dy == 0:
            return fext.at[:, pl.ds(own + H2, count), :], fext.at[:, pl.ds(land, count), :]
        side = 0 if dy == 1 else 1
        return s2s.at[side, :, pl.ds(own, count), :], s2r.at[side, :, pl.ds(land, count), :]

    def copy_of(stage, dx, dy):
        src, dst = ends(stage, dx, dy)
        k = stage * 8 + dirs.index((dx, dy))
        return pltpu.make_async_remote_copy(
            src_ref=src, dst_ref=dst, send_sem=ssem.at[k], recv_sem=rsem.at[k],
            device_id=(gx + dx, gy + dy), device_id_type=MESH)

    def start(stage, which):
        for dx, dy in which:
            @pl.when(exists(dx, dy))
            def _():
                copy_of(stage, dx, dy).start()

    def finish(stage, which):
        for dx, dy in which:
            @pl.when(exists(dx, dy))
            def _():
                copy_of(stage, dx, dy).wait_send()
        for dx, dy in which:
            @pl.when(exists(-dx, -dy))
            def _():
                copy_of(stage, dx, dy).wait_recv()

            @pl.when(jnp.logical_not(exists(-dx, -dy)))
            def _():
                dst = ends(stage, dx, dy)[1]
                dst[...] = jnp.zeros(dst.shape, f32)

    lane = lax.broadcasted_iota(jnp.int32, (8, T), 1)
    half = lax.rem(lane, 16) < 8

    local.wait()

    @pl.loop(0, ZIN // 4)
    def _(i):
        for u in range(4):
            z = 4 * i + u
            both = []
            for h in range(2):
                total = None
                for k in range(8):
                    v = iext[z, pl.ds(H1 + 8 * (8 * h + k), 8), :]
                    v = pltpu.roll(v, 16 * k + 8, 1)
                    total = v if k == 0 else jnp.where(lane >= 16 * k, v, total)
                both.append(total)
            s1s[0, z] = jnp.where(half, both[0], pltpu.roll(both[1], 8, 1))
            s1s[1, z] = jnp.where(half, pltpu.roll(both[0], T - 8, 1), both[1])

    for end, row in ((0, H1), (1, T)):
        for g in range(7):
            total = None
            for k in range(min(8, ZIN - 8 * g)):
                v = pltpu.roll(iext[8 * g + k, pl.ds(row, 8), :], 16 * k + 8, 1)
                total = v if k == 0 else jnp.where(lane >= 16 * k, v, total)
            c1s[end, g] = total

    kx = jnp.where(gx > 0, 1, 0) + jnp.where(gx < nx - 1, 1, 0)
    ky = jnp.where(gy > 0, 1, 0) + jnp.where(gy < ny - 1, 1, 0)
    pl.semaphore_wait(barrier, (kx + 1) * (ky + 1) - 1)
    start(0, dirs)

    def zfilter(load, zg, zd):
        v = [load(z) for z in range(2 * RD)]
        for z in range(0, ZG, 2):
            v.append(load(z + 2 * RD))
            v.append(load(z + 2 * RD + 1))
            w0, w1 = v[z:z + 2 * RD + 1], v[z + 1:z + 2 * RD + 2]
            for to, pair in ((zg, (fsym(g2, w0), fsym(g2, w1))), (zd, (fanti(d2, w0), fanti(d2, w1)))):
                high, low = split(jnp.concatenate(pair, axis=0))
                to[8 * z:8 * z + 16, :T] = high
                to[8 * z:8 * z + 16, T:] = low

    def yfilter(zg, zd, w2, wl, put):
        r = mm(zg[...], w2[...]) + mm(zg[:, :T], wl[...])
        put(0, r[:, :T].reshape(ZG, 8, T))
        put(2, r[:, T:].reshape(ZG, 8, T))
        r = mm(zd[...], w2[:, :T]) + mm(zd[:, :T], wl[:, :T])
        put(1, r.reshape(ZG, 8, T))

    def rows(t):
        return pl.ds(pl.multiple_of(t * 8, 8), 8)

    def zrow(t, zg, zd):
        zfilter(lambda z: iext[z, rows(t), :], zg, zd)

    def yrow(t, zg, zd):
        def put(f, value):
            (a1, a2, a3)[f][:, rows(t), :] = value
        yfilter(zg, zd, wyh, wyl, put)

    zrow(1, zg0, zd0)

    @pl.loop(0, 8)
    def _(i):
        t = 2 * i + 1
        yrow(t, zg0, zd0)
        zrow(t + 1, zg1, zd1)
        yrow(t + 1, zg1, zd1)
        zrow(jnp.minimum(t + 2, 16), zg0, zd0)

    finish(0, dirs)

    @pl.loop(0, ZIN // 13)
    def _(i):
        for u in range(13):
            z = 13 * i + u
            aux[0, z] = jnp.where(half, s1r[0, z], pltpu.roll(s1r[1, z], 8, 1))
            aux[1, z] = jnp.where(half, pltpu.roll(s1r[0, z], T - 8, 1), s1r[1, z])

    for g in range(7):
        top = jnp.where(half, c1r[0, 0, g], c1r[0, 1, g])
        bottom = jnp.where(half, c1r[1, 0, g], c1r[1, 1, g])
        for k in range(min(8, ZIN - 8 * g)):
            vt = pltpu.roll(top, (T - 16 * k) % T, 1) if k else top
            vb = pltpu.roll(bottom, (T + 16 - 16 * k) % T, 1) if k != 1 else bottom
            aux[2, 8 * g + k] = jnp.where(lane < 16, vt, vb)

    @pl.loop(0, 3)
    def _(n):
        def put(f, value):
            (e1, e2, e3)[f][n] = value
        zfilter(lambda z: aux[n, z], zg0, zd0)
        yfilter(zg0, zd0, weh, wel, put)

    zrow(0, zg0, zd0)
    yrow(0, zg0, zd0)
    zrow(17, zg1, zd1)
    yrow(17, zg1, zd1)

    outer = jnp.logical_or(lane < 8, lane >= T - 8)

    @pl.loop(0, 18)
    def _(t):
        n = jnp.where(jnp.logical_or(t == 0, t == 17), 2, jnp.where(t < 9, 0, 1))
        k = jnp.where(t == 0, 0, jnp.where(t == 17, 1, lax.rem(t + 7, 8)))
        for a, e in ((a1, e1), (a2, e2), (a3, e3)):
            for z in range(ZG):
                v = pltpu.roll(e[n, z], T - 8 - 16 * k, 1)
                a[z, rows(t), :] = a[z, rows(t), :] + jnp.where(outer, v, 0.0)

    slot = lax.rem(lane, 2 * S2) < S2

    def xtile(t):
        base = t * 8 + H1 - RD
        acc = [[None] * ZO for _ in range(6)]
        for z in range(ZG):
            gxv = fanti(d2, [a1[z, pl.ds(base + k, 8), :] for k in range(13)])
            gyv = fsym(g2, [a3[z, pl.ds(base + k, 8), :] for k in range(13)])
            gzv = fsym(g2, [a2[z, pl.ds(base + k, 8), :] for k in range(13)])
            prods = [gxv * gxv, gxv * gyv, gxv * gzv, gyv * gyv, gyv * gzv, gzv * gzv]
            for j in range(ZO):
                if 0 <= z - j <= 2 * RI:
                    for c in range(6):
                        term = g6[z - j] * prods[c]
                        acc[c][j] = term if acc[c][j] is None else acc[c][j] + term
        row = pl.ds(pl.multiple_of(t * 8, 8) + H2, 8)
        row0 = pl.ds(pl.multiple_of(t * 8, 8), 8)
        for j in range(ZO):
            both = []
            for h in range(2):
                total = None
                for k in range(3):
                    v = acc[3 * h + k][j]
                    fext[j * 6 + 3 * h + k, row, :] = v
                    v = pltpu.roll(v, 2 * S2 * k + S2, 1)
                    total = v if k == 0 else jnp.where(lane >= 2 * S2 * k, v, total)
                both.append(total)
            s2s[0, j, row0, :] = jnp.where(slot, both[0], pltpu.roll(both[1], S2, 1))
            s2s[1, j, row0, :] = jnp.where(slot, pltpu.roll(both[0], T - S2, 1), both[1])

    along_x = [d for d in dirs if d[1] == 0]
    beside = [d for d in dirs if d[1] != 0]

    @pl.loop(0, 6)
    def _(i):
        xtile(jnp.where(i < 3, i, 10 + i))

    start(1, along_x)

    @pl.loop(3, 13)
    def _(t):
        xtile(t)

    start(1, beside)
    finish(1, along_x)

    def xsmooth(value):
        high, low = split(value)
        return mm(sxh[...], high) + mm(sxh[...], low) + mm(sxl[...], high)

    @pl.loop(0, ZO)
    def _(j):
        for c in range(0, 6, 2):
            pair = []
            for n in range(2):
                high, low = split(fext[j * 6 + c + n])
                pair.append(mm2(high, low, syh[...], syl[...]))
            r = xsmooth(jnp.concatenate(pair, axis=1))
            o_ref[c, j] = r[:, :T]
            o_ref[c + 1, j] = r[:, T:]

    finish(1, beside)
    slot2 = lax.rem(lax.broadcasted_iota(jnp.int32, (X2, T), 1), 2 * S2) < S2
    lane2 = lax.broadcasted_iota(jnp.int32, (T, T), 1)
    outer2 = jnp.logical_or(lane2 < S2, lane2 >= T - S2)

    @pl.loop(0, ZO)
    def _(j):
        left, right = s2r[0, j], s2r[1, j]
        pair = []
        for value in (jnp.where(slot2, left, pltpu.roll(right, S2, 1)), jnp.where(slot2, pltpu.roll(left, T - S2, 1), right)):
            high, low = split(value)
            pair.append(mm2(high, low, seh[...], sel[...]))
        r = xsmooth(jnp.concatenate(pair, axis=1))
        for c in range(6):
            v = r[:, T * (c // 3):T * (c // 3) + T]
            v = pltpu.roll(v, T - S2 - 2 * S2 * (c % 3), 1)
            o_ref[c, j] = o_ref[c, j] + jnp.where(outer2, v, 0.0)


def shards(intensity):
    nx, ny = lax.axis_size("gx"), lax.axis_size("gy")
    f32, bf16 = jnp.float32, jnp.bfloat16
    vmem = pl.BlockSpec(memory_space=pltpu.VMEM)
    return pl.pallas_call(
        functools.partial(kernel, nx, ny),
        out_shape=jax.ShapeDtypeStruct((6, ZO, T, T), f32),
        in_specs=[pl.BlockSpec(memory_space=pl.ANY)] + [vmem] * 10,
        out_specs=vmem,
        scratch_shapes=[
            pltpu.VMEM((ZIN, X1, T), f32),
            pltpu.VMEM((2, ZIN, 8, T), f32),
            pltpu.VMEM((2, ZIN, 8, T), f32),
            pltpu.VMEM((2, 7, 8, T), f32),
            pltpu.VMEM((2, 2, 7, 8, T), f32),
            pltpu.VMEM((3, ZIN, 8, T), f32),
            pltpu.VMEM((ZG * 8, 2 * T), bf16),
            pltpu.VMEM((ZG * 8, 2 * T), bf16),
            pltpu.VMEM((ZG * 8, 2 * T), bf16),
            pltpu.VMEM((ZG * 8, 2 * T), bf16),
            pltpu.VMEM((ZG, X1, T), f32),
            pltpu.VMEM((ZG, X1, T), f32),
            pltpu.VMEM((ZG, X1, T), f32),
            pltpu.VMEM((3, ZG, 8, T), f32),
            pltpu.VMEM((3, ZG, 8, T), f32),
            pltpu.VMEM((3, ZG, 8, T), f32),
            pltpu.VMEM((6 * ZO, X2, T), f32),
            pltpu.VMEM((2, ZO, T, T), f32),
            pltpu.VMEM((2, ZO, X2, T), f32),
            pltpu.SemaphoreType.DMA,
            pltpu.SemaphoreType.DMA((16,)),
            pltpu.SemaphoreType.DMA((16,)),
        ],
        compiler_params=pltpu.CompilerParams(
            collective_id=0, has_side_effects=True, vmem_limit_bytes=56 * 1024 * 1024),
        cost_estimate=pl.CostEstimate(flops=4_000_000_000, bytes_accessed=6_000_000, transcendentals=0),
        name="structure_tensor",
    )(intensity, *weights())


def solution(mesh):
    in_specs = (P(None, "gx", "gy"),)
    out_specs = P(None, None, "gx", "gy")
    return jax.shard_map(shards, mesh=mesh, in_specs=in_specs, out_specs=out_specs, check_vma=False)
```

```python
import functools
import math

import jax
import jax.numpy as jnp
import ml_dtypes
import numpy as np
from jax import lax
from jax.experimental import pallas as pl
from jax.experimental.pallas import tpu as pltpu
from jax.sharding import PartitionSpec as P

RD = 6
RI = 18
ZIN = 52
ZG = ZIN - 2 * RD
ZO = ZG - 2 * RI
T = 128
H1 = 8
H2 = 24
X1 = T + 2 * H1
X2 = T + 2 * H2
S2 = 21
AHEAD = 2
MESH = pl.DeviceIdType.MESH


def gauss_taps(sigma, radius):
    values = [math.exp(-k * k / (2.0 * sigma * sigma)) for k in range(-radius, radius + 1)]
    total = sum(values)
    return [v / total for v in values]


def deriv_taps(sigma, radius):
    smooth = gauss_taps(sigma, radius)
    return [(k - radius) / (sigma * sigma) * smooth[k] for k in range(2 * radius + 1)]


def banded(positions, taps, count):
    radius = len(taps) // 2
    out = np.zeros((len(positions), count), np.float64)
    for row, pos in enumerate(positions):
        if pos is None:
            continue
        for col in range(max(0, pos - radius), min(count, pos + radius + 1)):
            out[row, col] = taps[pos - col + radius]
    return out


def split_const(matrix):
    high = matrix.astype(ml_dtypes.bfloat16)
    low = (matrix - high.astype(np.float64)).astype(ml_dtypes.bfloat16)
    return jnp.asarray(high), jnp.asarray(low)


def blocks(inside, outside, taps, count):
    radius = len(taps) // 2
    block = np.array([[taps[p - q + radius] if abs(p - q) <= radius else 0.0 for q in outside] for p in inside])
    out = np.zeros((T, T), np.float64)
    for k in range(count):
        n = len(inside)
        out[n * k:n * k + n, n * k:n * k + n] = block
    return out


def stacked(matrix):
    high, low = split_const(matrix)
    return jnp.concatenate([high, high], axis=0), low


def weights():
    g2, d2, g6 = gauss_taps(2.0, RD), deriv_taps(2.0, RD), gauss_taps(6.0, RI)
    own = list(range(T))
    wy = np.concatenate([banded(own, g2, T), banded(own, d2, T)], axis=1)
    near = list(range(-8, 0)) + list(range(T, T + 8))
    edge = list(range(T - 8, T)) + list(range(8))
    we = np.concatenate([blocks(near, edge, g2, 8), blocks(near, edge, d2, 8)], axis=1)
    sy = banded(own, g6, T)
    near = list(range(-S2, 0)) + list(range(T, T + S2))
    edge = list(range(T - S2, T)) + list(range(S2))
    se = blocks(near, edge, g6, 3)
    sx = banded(list(range(-H2, T + H2)), g6, T).T
    return stacked(wy) + stacked(we) + stacked(sy) + stacked(se) + split_const(sx)


def split(value):
    high = value.astype(jnp.bfloat16)
    low = (value - high.astype(jnp.float32)).astype(jnp.bfloat16)
    return high, low


def mm(a, b):
    return jnp.dot(a, b, preferred_element_type=jnp.float32)


def mm2(high, low, weight2, weight_low):
    return mm(jnp.concatenate([high, low], axis=1), weight2) + mm(high, weight_low)


def fsym(taps, values):
    r = len(taps) // 2
    total = taps[r] * values[r]
    for k in range(r):
        total = total + taps[k] * (values[k] + values[2 * r - k])
    return total


def fanti(taps, values):
    r = len(taps) // 2
    total = taps[2 * r] * (values[2 * r] - values[0])
    for k in range(1, r):
        total = total + taps[2 * r - k] * (values[2 * r - k] - values[k])
    return total


def toeplitz(taps):
    def tap(m):
        return taps[m] if 0 <= m < len(taps) else 0.0

    def add(acc, index, factor, value):
        if factor != 0.0:
            term = factor * value
            acc[index] = term if acc[index] is None else acc[index] + term

    def block(acc, first, middle, above, below, v0, v1):
        add(acc, first, middle, v0 + v1)
        add(acc, first + 1, above - middle, v1)
        add(acc, first + 2, below - middle, v0)

    def mix(q, v, acc):
        d = {s: tap(4 * q + s) for s in range(-3, 4)}
        block(acc, 0, d[0], d[1], d[-1], v[0] + v[2], v[1] + v[3])
        block(acc, 3, d[2] - d[0], d[3] - d[1], d[1] - d[-1], v[2], v[3])
        block(acc, 6, d[-2] - d[0], d[-1] - d[1], d[-3] - d[-1], v[0], v[1])

    return mix


def join(acc):
    m0, m1 = acc[0] + acc[1], acc[0] + acc[2]
    return [m0 + (acc[3] + acc[4]), m1 + (acc[3] + acc[5]), m0 + (acc[6] + acc[7]), m1 + (acc[6] + acc[8])]


def kernel(nx, ny, i_ref, wyh, wyl, weh, wel, syh, syl, seh, sel, sxh, sxl, o_ref,
           iext, s1s, s1r, c1s, c1r, aux, zg0, zd0, zg1, zd1, a1, a2, a3, b1, b2, b3, ec, en, ex, gc0, gc1,
           fext, s2s, s2r, lsem, ssem, rsem):
    gx, gy = lax.axis_index("gx"), lax.axis_index("gy")
    g2, d2, g6 = gauss_taps(2.0, RD), deriv_taps(2.0, RD), gauss_taps(6.0, RI)
    has = {-1: gx > 0, 1: gx < nx - 1}
    hasy = {-1: gy > 0, 1: gy < ny - 1}
    dirs = [(dx, dy) for dx in (-1, 0, 1) for dy in (-1, 0, 1) if dx or dy]
    f32 = jnp.float32

    def exists(dx, dy):
        cond = None
        if dx:
            cond = has[dx]
        if dy:
            cond = hasy[dy] if cond is None else jnp.logical_and(cond, hasy[dy])
        return cond

    def local(i):
        part = pl.ds(13 * i, 13)
        return pltpu.make_async_copy(i_ref.at[part], iext.at[part, H1:H1 + T, :], lsem.at[i])

    for i in range(4):
        local(i).start()

    barrier = pltpu.get_barrier_semaphore()
    for dx, dy in dirs:
        @pl.when(exists(dx, dy))
        def _():
            pl.semaphore_signal(barrier, inc=1, device_id=(gx + dx, gy + dy), device_id_type=MESH)

    pieces = [(0, H2), (T - H2, H2), (H2, 40), (H2 + 40, 40)]

    def ends(stage, dx, dy, piece):
        if stage == 0:
            own, land = {-1: (H1, T + H1), 1: (T, 0), 0: (0, 0)}[dx]
            if dy == 0:
                return iext.at[:, pl.ds(own, H1), :], iext.at[:, pl.ds(land, H1), :]
            if dx == 0:
                side = 0 if dy == 1 else 1
                return s1s.at[side], s1r.at[side]
            end = 0 if dx == -1 else 1
            return c1s.at[end], c1r.at[1 - end, 0 if dy == 1 else 1]
        own, land, count = {-1: (0, T + H2, H2), 1: (T - H2, 0, H2), 0: (0, H2, T)}[dx]
        if dy == 0:
            return fext.at[:, pl.ds(own + H2, count), :], fext.at[:, pl.ds(land, count), :]
        if dx == 0:
            own, count = pieces[piece]
            land = own + H2
        side = 0 if dy == 1 else 1
        return s2s.at[side, :, pl.ds(own, count), :], s2r.at[side, :, pl.ds(land, count), :]

    def copy_of(stage, dx, dy, piece=0):
        src, dst = ends(stage, dx, dy, piece)
        k = stage * 8 + dirs.index((dx, dy))
        if piece:
            k = 13 + piece * 2 + (0 if dy == 1 else 1) + 1
        return pltpu.make_async_remote_copy(
            src_ref=src, dst_ref=dst, send_sem=ssem.at[k], recv_sem=rsem.at[k],
            device_id=(gx + dx, gy + dy), device_id_type=MESH)

    def start(stage, which):
        for which_dir in which:
            @pl.when(exists(*which_dir[:2]))
            def _():
                copy_of(stage, *which_dir).start()

    def finish(stage, which):
        for which_dir in which:
            @pl.when(exists(*which_dir[:2]))
            def _():
                copy_of(stage, *which_dir).wait_send()
        for which_dir in which:
            dx, dy = which_dir[:2]

            @pl.when(exists(-dx, -dy))
            def _():
                copy_of(stage, *which_dir).wait_recv()

            @pl.when(jnp.logical_not(exists(-dx, -dy)))
            def _():
                dst = ends(stage, dx, dy, which_dir[2] if len(which_dir) > 2 else 0)[1]
                dst[...] = jnp.zeros(dst.shape, f32)

    lane = lax.broadcasted_iota(jnp.int32, (8, T), 1)
    half = lax.rem(lane, 16) < 8

    @pl.loop(0, 4)
    def _(i):
        local(i).wait()
        for u in range(13):
            z = 13 * i + u
            both = []
            for h in range(2):
                total = None
                for k in range(8):
                    v = iext[z, pl.ds(H1 + 8 * (8 * h + k), 8), :]
                    v = pltpu.roll(v, 16 * k + 8, 1)
                    total = v if k == 0 else jnp.where(lane >= 16 * k, v, total)
                both.append(total)
            s1s[0, z] = jnp.where(half, both[0], pltpu.roll(both[1], 8, 1))
            s1s[1, z] = jnp.where(half, pltpu.roll(both[0], T - 8, 1), both[1])

    for end, row in ((0, H1), (1, T)):
        for g in range(7):
            total = None
            for k in range(min(8, ZIN - 8 * g)):
                v = pltpu.roll(iext[8 * g + k, pl.ds(row, 8), :], 16 * k + 8, 1)
                total = v if k == 0 else jnp.where(lane >= 16 * k, v, total)
            c1s[end, g] = total

    def zfilter(load, zg, zd):
        v = [load(z) for z in range(2 * RD)]
        for z in range(0, ZG, 2):
            v.append(load(z + 2 * RD))
            v.append(load(z + 2 * RD + 1))
            w0, w1 = v[z:z + 2 * RD + 1], v[z + 1:z + 2 * RD + 2]
            for to, pair in ((zg, (fsym(g2, w0), fsym(g2, w1))), (zd, (fanti(d2, w0), fanti(d2, w1)))):
                high, low = split(jnp.concatenate(pair, axis=0))
                to[8 * z:8 * z + 16, :T] = high
                to[8 * z:8 * z + 16, T:] = low

    def yfilter(zg, zd, w2, wl, put):
        r = mm(zg[...], w2[...]) + mm(zg[:, :T], wl[...])
        put(0, r[:, :T].reshape(ZG, 8, T))
        put(2, r[:, T:].reshape(ZG, 8, T))
        r = mm(zd[...], w2[:, :T]) + mm(zd[:, :T], wl[:, :T])
        put(1, r.reshape(ZG, 8, T))

    def rows(t):
        return pl.ds(pl.multiple_of(t * 8, 8), 8)

    def zrow(t, zg, zd):
        zfilter(lambda z: iext[z, rows(t), :], zg, zd)

    def yrow(t, zg, zd):
        def put(f, value):
            (a1, a2, a3)[f][:, rows(t), :] = value
        yfilter(zg, zd, wyh, wyl, put)

    zrow(1, zg0, zd0)

    def pair(i):
        t = 2 * i + 1
        yrow(t, zg0, zd0)
        zrow(t + 1, zg1, zd1)
        yrow(t + 1, zg1, zd1)
        zrow(jnp.minimum(t + 2, 16), zg0, zd0)

    pl.loop(0, AHEAD)(pair)
    kx = jnp.where(gx > 0, 1, 0) + jnp.where(gx < nx - 1, 1, 0)
    ky = jnp.where(gy > 0, 1, 0) + jnp.where(gy < ny - 1, 1, 0)
    pl.semaphore_wait(barrier, (kx + 1) * (ky + 1) - 1)
    start(0, dirs)

    pl.loop(AHEAD, 8)(pair)

    def xfilters(r1, r2, r3):
        return fanti(d2, r1), fsym(g2, r3), fsym(g2, r2)

    def xtile(t):
        base = t * 8 + H1 - RD
        for z in range(ZG):
            r = [[a[z, pl.ds(base + k, 8), :] for k in range(2 * RD + 1)] for a in (a1, a2, a3)]
            for b, value in zip((b1, b2, b3), xfilters(*r)):
                b[t, z] = value

    @pl.loop(1, T // 8 - 1)
    def _(t):
        xtile(t)

    finish(0, dirs)

    @pl.loop(0, ZIN // 13)
    def _(i):
        for u in range(13):
            z = 13 * i + u
            aux[0, z] = jnp.where(half, s1r[0, z], pltpu.roll(s1r[1, z], 8, 1))
            aux[1, z] = jnp.where(half, pltpu.roll(s1r[0, z], T - 8, 1), s1r[1, z])

    for g in range(7):
        top = jnp.where(half, c1r[0, 0, g], c1r[0, 1, g])
        bottom = jnp.where(half, c1r[1, 0, g], c1r[1, 1, g])
        for k in range(min(8, ZIN - 8 * g)):
            vt = pltpu.roll(top, (T - 16 * k) % T, 1) if k else top
            vb = pltpu.roll(bottom, (T + 16 - 16 * k) % T, 1) if k != 1 else bottom
            aux[2, 8 * g + k] = jnp.where(lane < 16, vt, vb)

    def erow(n, zg, zd):
        def put(f, value):
            if n < 2:
                ec[f, n, :, 8:16, :] = value
            else:
                en[f] = value
        yfilter(zg, zd, weh, wel, put)

    zfilter(lambda z: aux[2, z], zg0, zd0)
    zfilter(lambda z: aux[0, z], zg1, zd1)
    erow(2, zg0, zd0)
    zfilter(lambda z: aux[1, z], zg0, zd0)
    erow(0, zg1, zd1)
    zrow(0, zg1, zd1)
    erow(1, zg0, zd0)
    zrow(17, zg0, zd0)
    yrow(0, zg1, zd1)
    yrow(17, zg0, zd0)

    @pl.loop(0, 2)
    def _(i):
        xtile(i * (T // 8 - 1))

    @pl.loop(0, ZG // 8)
    def _(i):
        for u in range(8):
            z = 8 * i + u
            for f in range(3):
                first, second, corner = ec[f, 0, z, 8:16, :], ec[f, 1, z, 8:16, :], en[f, z]
                down0, down1 = pltpu.roll(first, 16, 1), pltpu.roll(second, 16, 1)
                up0, up1 = pltpu.roll(first, T - 16, 1), pltpu.roll(second, T - 16, 1)
                ec[f, 0, z, 0:8, :] = jnp.where(lane < 16, corner, down0)
                ec[f, 1, z, 0:8, :] = jnp.where(lane < 16, down0, down1)
                ec[f, 0, z, 16:24, :] = jnp.where(lane < T - 16, up0, up1)
                ec[f, 1, z, 16:24, :] = jnp.where(lane < T - 16, up1, pltpu.roll(corner, T - 32, 1))

    @pl.loop(0, 2)
    def _(n):
        for z in range(ZG):
            r = [[ec[f, n, z, 8 - RD + k:16 - RD + k, :] for k in range(2 * RD + 1)] for f in range(3)]
            for f, value in enumerate(xfilters(*r)):
                ex[f, n, z] = value

    outer = jnp.logical_or(lane < 8, lane >= T - 8)
    slot = lax.rem(lane, 2 * S2) < S2
    mix = toeplitz(g6)

    def tile_of(i):
        return jnp.where(i < 3, i, jnp.where(i < 6, 10 + i, i - 3))

    def correct(i, gc):
        t = tile_of(i)
        n, k = t // 8, lax.rem(t, 8)
        for z in range(ZG):
            for f, b in enumerate((b1, b2, b3)):
                v = pltpu.roll(ex[f, n, z], T - 8 - 16 * k, 1)
                gc[f, z] = b[t, z] + jnp.where(outer, v, 0.0)

    def ptile(i, gc):
        row = pl.ds(pl.multiple_of(tile_of(i) * 8 + H2, 8), 8)
        for h, group in enumerate((((0, 0), (0, 1), (0, 2)), ((1, 1), (1, 2), (2, 2)))):
            acc = [[None] * 9 for _ in group]
            for q in range(ZG // 4):
                grads = {f: [gc[f, 4 * q + i] for i in range(4)] for f in sorted({f for pair in group for f in pair})}
                for pos, (f, g) in enumerate(group):
                    mix(q, [grads[f][i] * grads[g][i] for i in range(4)], acc[pos])
            for k in range(3):
                for j, v in enumerate(join(acc[k])):
                    fext[j * 6 + 3 * h + k, row, :] = v

    def pack(t):
        row = pl.ds(pl.multiple_of(t * 8 + H2, 8), 8)
        row0 = pl.ds(pl.multiple_of(t * 8, 8), 8)
        for j in range(ZO):
            both = []
            for h in range(2):
                total = None
                for k in range(3):
                    v = pltpu.roll(fext[j * 6 + 3 * h + k, row, :], 2 * S2 * k + S2, 1)
                    total = v if k == 0 else jnp.where(lane >= 2 * S2 * k, v, total)
                both.append(total)
            s2s[0, j, row0, :] = jnp.where(slot, both[0], pltpu.roll(both[1], S2, 1))
            s2s[1, j, row0, :] = jnp.where(slot, pltpu.roll(both[0], T - S2, 1), both[1])

    def two(i):
        correct(2 * i + 1, gc1)
        ptile(2 * i, gc0)
        correct(jnp.minimum(2 * i + 2, T // 8 - 1), gc0)
        ptile(2 * i + 1, gc1)

    along_x = [d for d in dirs if d[1] == 0]
    diagonal = [d for d in dirs if d[0] and d[1]]
    along_y = [[(0, -1, p), (0, 1, p)] for p in range(4)]

    correct(0, gc0)
    pl.loop(0, 3)(two)
    start(1, along_x)
    for t in (0, 1, 2, 13, 14, 15):
        pack(t)
    start(1, diagonal + along_y[0] + along_y[1])
    pl.loop(3, 6)(two)
    for t in range(3, 8):
        pack(t)
    start(1, along_y[2])
    pl.loop(6, 8)(two)
    for t in range(8, 13):
        pack(t)
    start(1, along_y[3])
    finish(1, along_x)


    def xsmooth(value):
        high, low = split(value)
        return mm(sxh[...], high) + mm(sxh[...], low) + mm(sxl[...], high)

    @pl.loop(0, ZO)
    def _(j):
        for c in range(0, 6, 2):
            r = xsmooth(jnp.concatenate([fext[j * 6 + c], fext[j * 6 + c + 1]], axis=1))
            high, low = split(r)
            for n in range(2):
                o_ref[c + n, j] = mm2(high[:, T * n:T * n + T], low[:, T * n:T * n + T], syh[...], syl[...])

    finish(1, diagonal + along_y[0] + along_y[1] + along_y[2] + along_y[3])
    slot2 = lax.rem(lax.broadcasted_iota(jnp.int32, (X2, T), 1), 2 * S2) < S2
    lane2 = lax.broadcasted_iota(jnp.int32, (T, T), 1)
    outer2 = jnp.logical_or(lane2 < S2, lane2 >= T - S2)

    for j in range(ZO):
        left, right = s2r[0, j], s2r[1, j]
        first = jnp.where(slot2, left, pltpu.roll(right, S2, 1))
        second = jnp.where(slot2, pltpu.roll(left, T - S2, 1), right)
        high, low = split(xsmooth(jnp.concatenate([first, second], axis=1)))
        for h in range(2):
            r = mm2(high[:, T * h:T * h + T], low[:, T * h:T * h + T], seh[...], sel[...])
            for k in range(3):
                v = pltpu.roll(r, T - S2 - 2 * S2 * k, 1)
                o_ref[3 * h + k, j] = o_ref[3 * h + k, j] + jnp.where(outer2, v, 0.0)


def shards(intensity):
    nx, ny = lax.axis_size("gx"), lax.axis_size("gy")
    f32, bf16 = jnp.float32, jnp.bfloat16
    vmem = pl.BlockSpec(memory_space=pltpu.VMEM)
    return pl.pallas_call(
        functools.partial(kernel, nx, ny),
        out_shape=jax.ShapeDtypeStruct((6, ZO, T, T), f32),
        in_specs=[pl.BlockSpec(memory_space=pl.ANY)] + [vmem] * 10,
        out_specs=vmem,
        scratch_shapes=[
            pltpu.VMEM((ZIN, X1, T), f32),
            pltpu.VMEM((2, ZIN, 8, T), f32),
            pltpu.VMEM((2, ZIN, 8, T), f32),
            pltpu.VMEM((2, 7, 8, T), f32),
            pltpu.VMEM((2, 2, 7, 8, T), f32),
            pltpu.VMEM((3, ZIN, 8, T), f32),
            pltpu.VMEM((ZG * 8, 2 * T), bf16),
            pltpu.VMEM((ZG * 8, 2 * T), bf16),
            pltpu.VMEM((ZG * 8, 2 * T), bf16),
            pltpu.VMEM((ZG * 8, 2 * T), bf16),
            pltpu.VMEM((ZG, X1, T), f32),
            pltpu.VMEM((ZG, X1, T), f32),
            pltpu.VMEM((ZG, X1, T), f32),
            pltpu.VMEM((T // 8, ZG, 8, T), f32),
            pltpu.VMEM((T // 8, ZG, 8, T), f32),
            pltpu.VMEM((T // 8, ZG, 8, T), f32),
            pltpu.VMEM((3, 2, ZG, 24, T), f32),
            pltpu.VMEM((3, ZG, 8, T), f32),
            pltpu.VMEM((3, 2, ZG, 8, T), f32),
            pltpu.VMEM((3, ZG, 8, T), f32),
            pltpu.VMEM((3, ZG, 8, T), f32),
            pltpu.VMEM((6 * ZO, X2, T), f32),
            pltpu.VMEM((2, ZO, T, T), f32),
            pltpu.VMEM((2, ZO, X2, T), f32),
            pltpu.SemaphoreType.DMA((4,)),
            pltpu.SemaphoreType.DMA((22,)),
            pltpu.SemaphoreType.DMA((22,)),
        ],
        compiler_params=pltpu.CompilerParams(
            collective_id=0, has_side_effects=True, vmem_limit_bytes=56 * 1024 * 1024),
        cost_estimate=pl.CostEstimate(flops=4_000_000_000, bytes_accessed=6_000_000, transcendentals=0),
        name="structure_tensor",
    )(intensity, *weights())


def solution(mesh):
    in_specs = (P(None, "gx", "gy"),)
    out_specs = P(None, None, "gx", "gy")
    return jax.shard_map(shards, mesh=mesh, in_specs=in_specs, out_specs=out_specs, check_vma=False)
```

```python
import functools
import math

import jax
import jax.numpy as jnp
import ml_dtypes
import numpy as np
from jax import lax
from jax.experimental import pallas as pl
from jax.experimental.pallas import tpu as pltpu
from jax.sharding import PartitionSpec as P

RD = 6
RI = 18
ZIN = 52
ZG = ZIN - 2 * RD
ZO = ZG - 2 * RI
T = 128
H1 = 8
H2 = 24
X1 = T + 2 * H1
X2 = T + 2 * H2
S2 = 21
MESH = pl.DeviceIdType.MESH


def gauss_taps(sigma, radius):
    values = [math.exp(-k * k / (2.0 * sigma * sigma)) for k in range(-radius, radius + 1)]
    total = sum(values)
    return [v / total for v in values]


def deriv_taps(sigma, radius):
    smooth = gauss_taps(sigma, radius)
    return [(k - radius) / (sigma * sigma) * smooth[k] for k in range(2 * radius + 1)]


def banded(positions, taps, count):
    radius = len(taps) // 2
    out = np.zeros((len(positions), count), np.float64)
    for row, pos in enumerate(positions):
        if pos is None:
            continue
        for col in range(max(0, pos - radius), min(count, pos + radius + 1)):
            out[row, col] = taps[pos - col + radius]
    return out


def split_const(matrix):
    high = matrix.astype(ml_dtypes.bfloat16)
    low = (matrix - high.astype(np.float64)).astype(ml_dtypes.bfloat16)
    return jnp.asarray(high), jnp.asarray(low)


def blocks(inside, outside, taps, count):
    radius = len(taps) // 2
    block = np.array([[taps[p - q + radius] if abs(p - q) <= radius else 0.0 for q in outside] for p in inside])
    out = np.zeros((T, T), np.float64)
    for k in range(count):
        n = len(inside)
        out[n * k:n * k + n, n * k:n * k + n] = block
    return out


def stacked(matrix):
    high, low = split_const(matrix)
    return jnp.concatenate([high, high], axis=0), low


def weights():
    g2, d2, g6 = gauss_taps(2.0, RD), deriv_taps(2.0, RD), gauss_taps(6.0, RI)
    own = list(range(T))
    wy = np.concatenate([banded(own, g2, T), banded(own, d2, T)], axis=1)
    near = list(range(-8, 0)) + list(range(T, T + 8))
    edge = list(range(T - 8, T)) + list(range(8))
    we = np.concatenate([blocks(near, edge, g2, 8), blocks(near, edge, d2, 8)], axis=1)
    sy = banded(own, g6, T)
    near = list(range(-S2, 0)) + list(range(T, T + S2))
    edge = list(range(T - S2, T)) + list(range(S2))
    se = blocks(near, edge, g6, 3)
    sx = banded(list(range(-H2, T + H2)), g6, T).T
    return stacked(wy) + stacked(we) + stacked(sy) + stacked(se) + split_const(sx)


def split(value):
    high = value.astype(jnp.bfloat16)
    low = (value - high.astype(jnp.float32)).astype(jnp.bfloat16)
    return high, low


def mm(a, b):
    return jnp.dot(a, b, preferred_element_type=jnp.float32)


def mm2(high, low, weight2, weight_low):
    return mm(jnp.concatenate([high, low], axis=1), weight2) + mm(high, weight_low)


def fsym(taps, values):
    r = len(taps) // 2
    total = taps[r] * values[r]
    for k in range(r):
        total = total + taps[k] * (values[k] + values[2 * r - k])
    return total


def fanti(taps, values):
    r = len(taps) // 2
    total = taps[2 * r] * (values[2 * r] - values[0])
    for k in range(1, r):
        total = total + taps[2 * r - k] * (values[2 * r - k] - values[k])
    return total


def toeplitz(taps):
    def tap(m):
        return taps[m] if 0 <= m < len(taps) else 0.0

    def add(acc, index, factor, value):
        if factor != 0.0:
            term = factor * value
            acc[index] = term if acc[index] is None else acc[index] + term

    def block(acc, first, middle, above, below, v0, v1):
        add(acc, first, middle, v0 + v1)
        add(acc, first + 1, above - middle, v1)
        add(acc, first + 2, below - middle, v0)

    def mix(q, v, acc):
        d = {s: tap(4 * q + s) for s in range(-3, 4)}
        block(acc, 0, d[0], d[1], d[-1], v[0] + v[2], v[1] + v[3])
        block(acc, 3, d[2] - d[0], d[3] - d[1], d[1] - d[-1], v[2], v[3])
        block(acc, 6, d[-2] - d[0], d[-1] - d[1], d[-3] - d[-1], v[0], v[1])

    return mix


def join(acc):
    m0, m1 = acc[0] + acc[1], acc[0] + acc[2]
    return [m0 + (acc[3] + acc[4]), m1 + (acc[3] + acc[5]), m0 + (acc[6] + acc[7]), m1 + (acc[6] + acc[8])]


def kernel(nx, ny, i_ref, wyh, wyl, weh, wel, syh, syl, seh, sel, sxh, sxl, o_ref,
           iext, s1s, s1r, c1s, c1r, aux, zg0, zd0, zg1, zd1, a1, a2, a3, b1, b2, b3, ec, en, ex, gc0, gc1,
           fext, s2s, s2r, lsem, ssem, rsem):
    gx, gy = lax.axis_index("gx"), lax.axis_index("gy")
    g2, d2, g6 = gauss_taps(2.0, RD), deriv_taps(2.0, RD), gauss_taps(6.0, RI)
    has = {-1: gx > 0, 1: gx < nx - 1}
    hasy = {-1: gy > 0, 1: gy < ny - 1}
    dirs = [(dx, dy) for dx in (-1, 0, 1) for dy in (-1, 0, 1) if dx or dy]
    f32 = jnp.float32

    def exists(dx, dy):
        cond = None
        if dx:
            cond = has[dx]
        if dy:
            cond = hasy[dy] if cond is None else jnp.logical_and(cond, hasy[dy])
        return cond

    def local(i):
        part = pl.ds(13 * i, 13)
        return pltpu.make_async_copy(i_ref.at[part], iext.at[part, H1:H1 + T, :], lsem.at[i])

    for i in range(4):
        local(i).start()

    barrier = pltpu.get_barrier_semaphore()
    for dx, dy in dirs:
        @pl.when(exists(dx, dy))
        def _():
            pl.semaphore_signal(barrier, inc=1, device_id=(gx + dx, gy + dy), device_id_type=MESH)

    pieces = [(0, H2), (T - H2, H2), (H2, 40), (H2 + 40, 40)]

    def ends(stage, dx, dy, piece):
        if stage == 0:
            own, land = {-1: (H1, T + H1), 1: (T, 0), 0: (0, 0)}[dx]
            if dy == 0:
                return iext.at[:, pl.ds(own, H1), :], iext.at[:, pl.ds(land, H1), :]
            if dx == 0:
                side = 0 if dy == 1 else 1
                return s1s.at[side], s1r.at[side]
            end = 0 if dx == -1 else 1
            return c1s.at[end], c1r.at[1 - end, 0 if dy == 1 else 1]
        own, land, count = {-1: (0, T + H2, H2), 1: (T - H2, 0, H2), 0: (0, H2, T)}[dx]
        if dy == 0:
            return fext.at[:, pl.ds(own + H2, count), :], fext.at[:, pl.ds(land, count), :]
        if dx == 0:
            own, count = pieces[piece]
            land = own + H2
        side = 0 if dy == 1 else 1
        return s2s.at[side, :, pl.ds(own, count), :], s2r.at[side, :, pl.ds(land, count), :]

    def copy_of(stage, dx, dy, piece=0):
        src, dst = ends(stage, dx, dy, piece)
        k = stage * 8 + dirs.index((dx, dy))
        if piece:
            k = 13 + piece * 2 + (0 if dy == 1 else 1) + 1
        return pltpu.make_async_remote_copy(
            src_ref=src, dst_ref=dst, send_sem=ssem.at[k], recv_sem=rsem.at[k],
            device_id=(gx + dx, gy + dy), device_id_type=MESH)

    def start(stage, which):
        for which_dir in which:
            @pl.when(exists(*which_dir[:2]))
            def _():
                copy_of(stage, *which_dir).start()

    def finish(stage, which):
        for which_dir in which:
            @pl.when(exists(*which_dir[:2]))
            def _():
                copy_of(stage, *which_dir).wait_send()
        for which_dir in which:
            dx, dy = which_dir[:2]

            @pl.when(exists(-dx, -dy))
            def _():
                copy_of(stage, *which_dir).wait_recv()

            @pl.when(jnp.logical_not(exists(-dx, -dy)))
            def _():
                dst = ends(stage, dx, dy, which_dir[2] if len(which_dir) > 2 else 0)[1]
                dst[...] = jnp.zeros(dst.shape, f32)

    lane = lax.broadcasted_iota(jnp.int32, (8, T), 1)
    half = lax.rem(lane, 16) < 8

    @pl.loop(0, 4)
    def _(i):
        local(i).wait()
        for u in range(13):
            z = 13 * i + u
            both = []
            for h in range(2):
                total = None
                for k in range(8):
                    v = iext[z, pl.ds(H1 + 8 * (8 * h + k), 8), :]
                    v = pltpu.roll(v, 16 * k + 8, 1)
                    total = v if k == 0 else jnp.where(lane >= 16 * k, v, total)
                both.append(total)
            s1s[0, z] = jnp.where(half, both[0], pltpu.roll(both[1], 8, 1))
            s1s[1, z] = jnp.where(half, pltpu.roll(both[0], T - 8, 1), both[1])

    for end, row in ((0, H1), (1, T)):
        for g in range(7):
            total = None
            for k in range(min(8, ZIN - 8 * g)):
                v = pltpu.roll(iext[8 * g + k, pl.ds(row, 8), :], 16 * k + 8, 1)
                total = v if k == 0 else jnp.where(lane >= 16 * k, v, total)
            c1s[end, g] = total

    def zfilter(load, zg, zd):
        v = [load(z) for z in range(2 * RD)]
        for z in range(0, ZG, 2):
            v.append(load(z + 2 * RD))
            v.append(load(z + 2 * RD + 1))
            w0, w1 = v[z:z + 2 * RD + 1], v[z + 1:z + 2 * RD + 2]
            for to, pair in ((zg, (fsym(g2, w0), fsym(g2, w1))), (zd, (fanti(d2, w0), fanti(d2, w1)))):
                high, low = split(jnp.concatenate(pair, axis=0))
                to[8 * z:8 * z + 16, :T] = high
                to[8 * z:8 * z + 16, T:] = low

    def yfilter(zg, zd, w2, wl, put):
        r = mm(zg[...], w2[...]) + mm(zg[:, :T], wl[...])
        put(0, r[:, :T].reshape(ZG, 8, T))
        put(2, r[:, T:].reshape(ZG, 8, T))
        r = mm(zd[...], w2[:, :T]) + mm(zd[:, :T], wl[:, :T])
        put(1, r.reshape(ZG, 8, T))

    def rows(t):
        return pl.ds(pl.multiple_of(t * 8, 8), 8)

    def zrow(t, zg, zd):
        zfilter(lambda z: iext[z, rows(t), :], zg, zd)

    def yrow(t, zg, zd):
        def put(f, value):
            (a1, a2, a3)[f][:, rows(t), :] = value
        yfilter(zg, zd, wyh, wyl, put)

    zrow(1, zg0, zd0)

    def pair(i):
        t = 2 * i + 1
        yrow(t, zg0, zd0)
        zrow(t + 1, zg1, zd1)
        yrow(t + 1, zg1, zd1)
        zrow(jnp.minimum(t + 2, 16), zg0, zd0)

    along_x = [d for d in dirs if d[1] == 0]
    diagonal = [d for d in dirs if d[0] and d[1]]
    kx = jnp.where(gx > 0, 1, 0) + jnp.where(gx < nx - 1, 1, 0)
    ky = jnp.where(gy > 0, 1, 0) + jnp.where(gy < ny - 1, 1, 0)
    pl.semaphore_wait(barrier, (kx + 1) * (ky + 1) - 1)
    start(0, along_x + [(0, -1), (0, 1)] + diagonal)

    pl.loop(0, 8)(pair)

    def xfilters(r1, r2, r3):
        return fanti(d2, r1), fsym(g2, r3), fsym(g2, r2)

    def xtile(t):
        base = t * 8 + H1 - RD
        for z in range(ZG):
            r = [[a[z, pl.ds(base + k, 8), :] for k in range(2 * RD + 1)] for a in (a1, a2, a3)]
            for b, value in zip((b1, b2, b3), xfilters(*r)):
                b[t, z] = value

    @pl.loop(1, T // 8 - 1)
    def _(t):
        xtile(t)

    finish(0, dirs)

    @pl.loop(0, ZIN // 13)
    def _(i):
        for u in range(13):
            z = 13 * i + u
            aux[0, z] = jnp.where(half, s1r[0, z], pltpu.roll(s1r[1, z], 8, 1))
            aux[1, z] = jnp.where(half, pltpu.roll(s1r[0, z], T - 8, 1), s1r[1, z])

    for g in range(7):
        top = jnp.where(half, c1r[0, 0, g], c1r[0, 1, g])
        bottom = jnp.where(half, c1r[1, 0, g], c1r[1, 1, g])
        for k in range(min(8, ZIN - 8 * g)):
            vt = pltpu.roll(top, (T - 16 * k) % T, 1) if k else top
            vb = pltpu.roll(bottom, (T + 16 - 16 * k) % T, 1) if k != 1 else bottom
            aux[2, 8 * g + k] = jnp.where(lane < 16, vt, vb)

    def erow(n, zg, zd):
        def put(f, value):
            if n < 2:
                ec[f, n, :, 8:16, :] = value
            else:
                en[f] = value
        yfilter(zg, zd, weh, wel, put)

    zfilter(lambda z: aux[2, z], zg0, zd0)
    zfilter(lambda z: aux[0, z], zg1, zd1)
    erow(2, zg0, zd0)
    zfilter(lambda z: aux[1, z], zg0, zd0)
    erow(0, zg1, zd1)
    zrow(0, zg1, zd1)
    erow(1, zg0, zd0)
    zrow(17, zg0, zd0)
    yrow(0, zg1, zd1)
    yrow(17, zg0, zd0)

    @pl.loop(0, 2)
    def _(i):
        xtile(i * (T // 8 - 1))

    @pl.loop(0, ZG // 8)
    def _(i):
        for u in range(8):
            z = 8 * i + u
            for f in range(3):
                first, second, corner = ec[f, 0, z, 8:16, :], ec[f, 1, z, 8:16, :], en[f, z]
                down0, down1 = pltpu.roll(first, 16, 1), pltpu.roll(second, 16, 1)
                up0, up1 = pltpu.roll(first, T - 16, 1), pltpu.roll(second, T - 16, 1)
                ec[f, 0, z, 0:8, :] = jnp.where(lane < 16, corner, down0)
                ec[f, 1, z, 0:8, :] = jnp.where(lane < 16, down0, down1)
                ec[f, 0, z, 16:24, :] = jnp.where(lane < T - 16, up0, up1)
                ec[f, 1, z, 16:24, :] = jnp.where(lane < T - 16, up1, pltpu.roll(corner, T - 32, 1))

    @pl.loop(0, 2)
    def _(n):
        for z in range(ZG):
            r = [[ec[f, n, z, 8 - RD + k:16 - RD + k, :] for k in range(2 * RD + 1)] for f in range(3)]
            for f, value in enumerate(xfilters(*r)):
                ex[f, n, z] = value

    outer = jnp.logical_or(lane < 8, lane >= T - 8)
    slot = lax.rem(lane, 2 * S2) < S2
    mix = toeplitz(g6)

    def tile_of(i):
        return jnp.where(i < 3, i, jnp.where(i < 6, 10 + i, i - 3))

    def correct(i, gc):
        t = tile_of(i)
        n, k = t // 8, lax.rem(t, 8)
        for z in range(ZG):
            for f, b in enumerate((b1, b2, b3)):
                v = pltpu.roll(ex[f, n, z], T - 8 - 16 * k, 1)
                gc[f, z] = b[t, z] + jnp.where(outer, v, 0.0)

    def ptile(i, gc):
        row = pl.ds(pl.multiple_of(tile_of(i) * 8 + H2, 8), 8)
        for h, group in enumerate((((0, 0), (0, 1), (0, 2)), ((1, 1), (1, 2), (2, 2)))):
            acc = [[None] * 9 for _ in group]
            for q in range(ZG // 4):
                grads = {f: [gc[f, 4 * q + i] for i in range(4)] for f in sorted({f for pair in group for f in pair})}
                for pos, (f, g) in enumerate(group):
                    mix(q, [grads[f][i] * grads[g][i] for i in range(4)], acc[pos])
            for k in range(3):
                for j, v in enumerate(join(acc[k])):
                    fext[j * 6 + 3 * h + k, row, :] = v

    def pack(t):
        row = pl.ds(pl.multiple_of(t * 8 + H2, 8), 8)
        row0 = pl.ds(pl.multiple_of(t * 8, 8), 8)
        for j in range(ZO):
            both = []
            for h in range(2):
                total = None
                for k in range(3):
                    v = pltpu.roll(fext[j * 6 + 3 * h + k, row, :], 2 * S2 * k + S2, 1)
                    total = v if k == 0 else jnp.where(lane >= 2 * S2 * k, v, total)
                both.append(total)
            s2s[0, j, row0, :] = jnp.where(slot, both[0], pltpu.roll(both[1], S2, 1))
            s2s[1, j, row0, :] = jnp.where(slot, pltpu.roll(both[0], T - S2, 1), both[1])

    def two(i):
        correct(2 * i + 1, gc1)
        ptile(2 * i, gc0)
        correct(jnp.minimum(2 * i + 2, T // 8 - 1), gc0)
        ptile(2 * i + 1, gc1)

    along_y = [[(0, -1, p), (0, 1, p)] for p in range(4)]

    correct(0, gc0)
    pl.loop(0, 3)(two)
    start(1, along_x)
    for t in (0, 1, 2, 13, 14, 15):
        pack(t)
    start(1, diagonal + along_y[0] + along_y[1])
    pl.loop(3, 6)(two)
    for t in range(3, 8):
        pack(t)
    start(1, along_y[2])
    pl.loop(6, 8)(two)
    for t in range(8, 13):
        pack(t)
    start(1, along_y[3])
    finish(1, along_x)


    def xsmooth(value):
        high, low = split(value)
        return mm(sxh[...], high) + mm(sxh[...], low) + mm(sxl[...], high)

    @pl.loop(0, ZO)
    def _(j):
        for c in range(0, 6, 2):
            r = xsmooth(jnp.concatenate([fext[j * 6 + c], fext[j * 6 + c + 1]], axis=1))
            high, low = split(r)
            for n in range(2):
                o_ref[c + n, j] = mm2(high[:, T * n:T * n + T], low[:, T * n:T * n + T], syh[...], syl[...])

    finish(1, diagonal + along_y[0] + along_y[1] + along_y[2] + along_y[3])
    slot2 = lax.rem(lax.broadcasted_iota(jnp.int32, (X2, T), 1), 2 * S2) < S2
    lane2 = lax.broadcasted_iota(jnp.int32, (T, T), 1)
    outer2 = jnp.logical_or(lane2 < S2, lane2 >= T - S2)

    for j in range(ZO):
        left, right = s2r[0, j], s2r[1, j]
        first = jnp.where(slot2, left, pltpu.roll(right, S2, 1))
        second = jnp.where(slot2, pltpu.roll(left, T - S2, 1), right)
        high, low = split(xsmooth(jnp.concatenate([first, second], axis=1)))
        for h in range(2):
            r = mm2(high[:, T * h:T * h + T], low[:, T * h:T * h + T], seh[...], sel[...])
            for k in range(3):
                v = pltpu.roll(r, T - S2 - 2 * S2 * k, 1)
                o_ref[3 * h + k, j] = o_ref[3 * h + k, j] + jnp.where(outer2, v, 0.0)


def shards(intensity):
    nx, ny = lax.axis_size("gx"), lax.axis_size("gy")
    f32, bf16 = jnp.float32, jnp.bfloat16
    vmem = pl.BlockSpec(memory_space=pltpu.VMEM)
    return pl.pallas_call(
        functools.partial(kernel, nx, ny),
        out_shape=jax.ShapeDtypeStruct((6, ZO, T, T), f32),
        in_specs=[pl.BlockSpec(memory_space=pl.ANY)] + [vmem] * 10,
        out_specs=vmem,
        scratch_shapes=[
            pltpu.VMEM((ZIN, X1, T), f32),
            pltpu.VMEM((2, ZIN, 8, T), f32),
            pltpu.VMEM((2, ZIN, 8, T), f32),
            pltpu.VMEM((2, 7, 8, T), f32),
            pltpu.VMEM((2, 2, 7, 8, T), f32),
            pltpu.VMEM((3, ZIN, 8, T), f32),
            pltpu.VMEM((ZG * 8, 2 * T), bf16),
            pltpu.VMEM((ZG * 8, 2 * T), bf16),
            pltpu.VMEM((ZG * 8, 2 * T), bf16),
            pltpu.VMEM((ZG * 8, 2 * T), bf16),
            pltpu.VMEM((ZG, X1, T), f32),
            pltpu.VMEM((ZG, X1, T), f32),
            pltpu.VMEM((ZG, X1, T), f32),
            pltpu.VMEM((T // 8, ZG, 8, T), f32),
            pltpu.VMEM((T // 8, ZG, 8, T), f32),
            pltpu.VMEM((T // 8, ZG, 8, T), f32),
            pltpu.VMEM((3, 2, ZG, 24, T), f32),
            pltpu.VMEM((3, ZG, 8, T), f32),
            pltpu.VMEM((3, 2, ZG, 8, T), f32),
            pltpu.VMEM((3, ZG, 8, T), f32),
            pltpu.VMEM((3, ZG, 8, T), f32),
            pltpu.VMEM((6 * ZO, X2, T), f32),
            pltpu.VMEM((2, ZO, T, T), f32),
            pltpu.VMEM((2, ZO, X2, T), f32),
            pltpu.SemaphoreType.DMA((4,)),
            pltpu.SemaphoreType.DMA((22,)),
            pltpu.SemaphoreType.DMA((22,)),
        ],
        compiler_params=pltpu.CompilerParams(
            collective_id=0, has_side_effects=True, vmem_limit_bytes=56 * 1024 * 1024),
        cost_estimate=pl.CostEstimate(flops=4_000_000_000, bytes_accessed=6_000_000, transcendentals=0),
        name="structure_tensor",
    )(intensity, *weights())


def solution(mesh):
    in_specs = (P(None, "gx", "gy"),)
    out_specs = P(None, None, "gx", "gy")
    return jax.shard_map(shards, mesh=mesh, in_specs=in_specs, out_specs=out_specs, check_vma=False)
```
